32 devices in a mesh: src: 8 (over z, x), tgt: 4 (over y, core).
Axes of the slice: x: 2, y: 2, z: 4, core: 2. Of those that a mesh axis runs over, the one named last changes fastest.
Arguments:
- src_feat: bfloat16 [16384, 768], P(('src', 'tgt')), may hold values from -6 to 6
- tgt_feat: bfloat16 [8192, 768], P(('tgt', 'src')), may hold values from -6 to 6
- rel_weight: bfloat16 [3, 768, 1024], replicated, may hold values from -0.21875 to 0.21875
- self_weight: bfloat16 [768, 1024], replicated, may hold values from -0.21875 to 0.21875
- adj_weight: bfloat16 [8, 64, 4, 128, 128], P('src', 'tgt'), may hold values from 0 to 0.026977539
- adj_source: int32 [8, 64, 4], P('src', 'tgt'), may hold values from 0 to 47
- adj_count: int32 [8, 64], P('src', 'tgt'), may hold values from 1 to 4
Outputs:
- hidden_out: bfloat16 [8192, 1024], P(('tgt', 'src'))
The draws below stay inside these ranges and needn't reach their ends.
All inputs are finite; a program needn't handle non-finite values.
Results may differ from the reference program's by a relative error of at most 0.004.
Values may be sent and summed in bfloat16 or wider, within the bound.
A program may use at most 128 MiB of HBM per device.

```python
import math
import jax
import jax.numpy as jnp
import numpy as np
from jax import lax

D = 768
HID = 1024
REL = 3
BLK = 128
KSLOT = 4
SRC_DEV = 2048
SOURCES = 16384
TBLOCKS = 64
TARGETS = 8192
N_SRC = 8


def plant(array, own_key, least, largest):
    spot = [jax.random.randint(jax.random.fold_in(own_key, axis), (), 0, length) for axis, length in enumerate(array.shape)]
    longest = array.shape.index(max(array.shape))
    beside = spot[:longest] + [(spot[longest] + 1) % array.shape[longest]] + spot[longest + 1:]
    return array.at[tuple(spot)].set(least).at[tuple(beside)].set(largest)


def shard_levels(key, extent, shards, smallest, top_value):
    loudness, own = 1.0, jax.random.fold_in(key, 6)
    for position, blocks in shards:
        steps = jnp.exp(jax.random.uniform(jax.random.fold_in(own, position), (blocks,), jnp.float32, smallest / len(shards), top_value / len(shards)))
        loudness = loudness * jnp.repeat(steps, extent[position] // blocks).reshape([-1 if axis == position else 1 for axis in range(len(extent))])
    return loudness


def cumulative_ranks(count, skew):
    weights = [(1 << 20) // math.isqrt(standing ** skew) + 1 for standing in range(1, count + 1)]
    spread = 1 + sum(weights) // (1 << 30)
    return np.cumsum(np.array([max(1, weight // spread) for weight in weights]))


def skewed_ids(key, shape, number_of, slope):
    grid = cumulative_ranks(number_of, slope)
    pick = jax.random.randint(jax.random.fold_in(key, 1), shape, 0, int(grid[number_of - 1]))
    rank = jnp.searchsorted(jnp.asarray(grid, jnp.int32), pick, side="right")
    return jax.random.permutation(jax.random.fold_in(key, 2), number_of)[rank].astype(jnp.int32)


def scatter_about(rng, dims, scale, most, split=(), kind=jnp.bfloat16):
    values = jax.random.normal(rng, dims, jnp.float32) * scale
    if len(split) > 0:
        values = shard_levels(rng, dims, split, -0.22, 0.18) * values
    return jnp.clip(values, min=-most, max=most).astype(kind)


def setup_inputs(seed: int = 0) -> dict:
    splits = jax.random.split(jax.random.key(seed), 8)
    src_feat = scatter_about(splits[0], (SOURCES, D), 1.0, 6.0, ((0, 32),))
    tgt_feat = scatter_about(splits[1], (TARGETS, D), 1.0, 6.0, ((0, 32),))
    rel_weight = scatter_about(splits[2], (REL, D, HID), D ** -0.5, 0.21875)
    self_weight = scatter_about(splits[3], (D, HID), D ** -0.5, 0.21875)
    adj_weight = jnp.clip(0.026977539 * jax.random.uniform(splits[4], (N_SRC, TBLOCKS, KSLOT, BLK, BLK), jnp.float32) ** shard_levels(splits[4], (N_SRC, TBLOCKS, KSLOT, BLK, BLK), ((0, 8), (1, 4)), -0.2, 0.2), 0.0, 0.026977539).astype(jnp.bfloat16)
    adj_source = plant(skewed_ids(splits[5], (N_SRC, TBLOCKS, KSLOT), REL * SRC_DEV // BLK, 2), jax.random.fold_in(splits[5], 3), 0, (REL * SRC_DEV // BLK) - 1).astype(jnp.int32)
    adj_count = plant(jax.random.randint(splits[6], (N_SRC, TBLOCKS), 1, KSLOT + 1), jax.random.fold_in(splits[6], 1), 1, KSLOT).astype(jnp.int32)
    return dict(src_feat=src_feat, tgt_feat=tgt_feat, rel_weight=rel_weight, self_weight=self_weight, adj_weight=adj_weight, adj_source=adj_source, adj_count=adj_count)


def reference(src_feat, tgt_feat, rel_weight, self_weight, adj_weight, adj_source, adj_count):
    features = src_feat.reshape(N_SRC, SRC_DEV, D)
    slot_iota = jnp.arange(KSLOT, dtype=jnp.int32)

    def per_device(running, inputs):
        src_rows, weights, source_index, count_live = inputs
        transformed = jnp.einsum("nd,rdh->rnh", src_rows.astype(jnp.float32), rel_weight.astype(jnp.float32)).astype(jnp.bfloat16)
        transformed = transformed.reshape(REL * (SRC_DEV // BLK), BLK, HID)
        picked = transformed[source_index]
        alive_mask = slot_iota[None, :] < count_live[:, None]
        live_weight = jnp.where(alive_mask[:, :, None, None], weights, jnp.zeros_like(weights))
        partial_value = jnp.einsum("tkij,tkjh->tih", live_weight.astype(jnp.float32), picked.astype(jnp.float32))
        return running + partial_value, None

    start = jnp.zeros((TBLOCKS, BLK, HID), jnp.float32)
    summed, _ = lax.scan(per_device, start, (features, adj_weight, adj_source, adj_count))
    summed = summed.reshape(TARGETS, HID)
    self_term = jnp.dot(tgt_feat, self_weight, preferred_element_type=jnp.float32)
    return jax.nn.relu(summed + self_term).astype(jnp.bfloat16)
```

```python
import functools

import jax
import jax.numpy as jnp
from jax import lax
from jax.experimental import pallas as pl
from jax.experimental.pallas import tpu as pltpu
from jax.sharding import PartitionSpec as P

BLK = 128
TILE = 256
F32 = jnp.float32
BF16 = jnp.bfloat16


def kernel(n_src, n_tgt, cuts,
           feat, tgt, rel, selfw, adj, index, count, out,
           gath, rel_v, self_v, tgt_v, adj_v, trans, self_acc, peer_msg, own_msg, x_in, up_in, down_in, z_out,
           load_sem, y_send, y_recv, c_send, c_recv, f_send, f_recv, x_send, x_recv, z_send, up_recv, down_recv):
    s, t = lax.axis_index("src"), lax.axis_index("tgt")
    x, z = s % 2, s // 2
    n_z = n_src // 2
    n_y = n_tgt // 2
    mate = t + 1 - 2 * (t % 2)
    x_peer = s + 1 - 2 * x
    rows, rels, hid = gath.shape[1], rel_v.shape[0], rel_v.shape[2]
    per_rel = trans.shape[0] // rels
    tblocks, slots = adj_v.shape[0], adj_v.shape[1]
    pieces, piece = z_out.shape[1], z_out.shape[2]
    owned = pieces * piece
    cut = rows // cuts
    tiles = hid // TILE

    def to(src_ref, dst_ref, send, recv, **where):
        return pltpu.make_async_remote_copy(
            src_ref=src_ref, dst_ref=dst_ref, send_sem=send, recv_sem=recv,
            device_id=where, device_id_type=pl.DeviceIdType.MESH)

    loads = [
        pltpu.make_async_copy(feat, gath.at[t], load_sem.at[0]),
        pltpu.make_async_copy(rel, rel_v, load_sem.at[1]),
        pltpu.make_async_copy(tgt, tgt_v, load_sem.at[2]),
        pltpu.make_async_copy(selfw, self_v, load_sem.at[3]),
        pltpu.make_async_copy(adj.at[0], adj_v, load_sem.at[4]),
    ]
    for load in loads:
        load.start()

    barrier = pltpu.get_barrier_semaphore()

    def greet(**where):
        pl.semaphore_signal(barrier, inc=1, device_id=where, device_id_type=pl.DeviceIdType.MESH)

    greet(tgt=mate)
    greet(src=x_peer)
    for j in range(1, n_y):
        greet(tgt=(t + 2 * j) % n_tgt)
    pl.when(z > 0)(lambda: greet(src=s - 2))
    pl.when(z < n_z - 1)(lambda: greet(src=s + 2))
    pl.semaphore_wait(barrier, n_y + 1 + jnp.minimum(z, 1) + jnp.minimum(n_z - 1 - z, 1))

    def y_copy(j, p, owner, peer):
        spot = pl.ds(p * cut, cut)
        return to(feat.at[spot], gath.at[owner, spot], y_send.at[j - 1, p], y_recv.at[j - 1, p], tgt=peer)

    def f_copy(j, p, owner):
        here = gath.at[owner, pl.ds(p * cut, cut)]
        return to(here, here, f_send.at[j - 1, p], f_recv.at[j - 1, p], tgt=mate)

    for p in range(cuts):
        for j in range(1, n_y):
            y_copy(j, p, t, (t + 2 * j) % n_tgt).start()
    mate_copy = to(feat, gath.at[t], c_send, c_recv, tgt=mate)
    mate_copy.start()

    def transform(owner, first, many):
        block = (owner * rows + first) // BLK

        @pl.loop(0, rels)
        def _(r):
            @pl.loop(0, tiles)
            def _(c):
                col = pl.ds(pl.multiple_of(c * TILE, TILE), TILE)
                made = jnp.dot(gath[owner, pl.ds(first, many), :], rel_v[r, :, col], preferred_element_type=F32)
                trans[pl.ds(r * per_rel + block, many // BLK), :, col] = made.astype(BF16).reshape(many // BLK, BLK, TILE)

    loads[0].wait()
    loads[1].wait()
    transform(t, 0, rows)
    mate_copy.wait_recv()
    transform(mate, 0, rows)
    loads[2].wait()
    loads[3].wait()
    loads[4].wait()

    @pl.loop(0, tiles)
    def _(c):
        col = pl.ds(pl.multiple_of(c * TILE, TILE), TILE)
        made = jnp.dot(tgt_v[...], self_v[:, col], preferred_element_type=F32)
        self_acc[:, :, col] = made.reshape(pieces, piece, TILE)

    for p in range(cuts):
        for j in range(1, n_y):
            owner = (t - 2 * j + n_tgt) % n_tgt
            y_copy(j, p, owner, owner).wait_recv()
            f_copy(j, p, owner).start()
            transform(owner, p * cut, cut)
        for j in range(1, n_y):
            owner = (mate - 2 * j + n_tgt) % n_tgt
            f_copy(j, p, owner).wait_recv()
            transform(owner, p * cut, cut)

    def message(block, store):
        live = [
            (adj_v[block, k].astype(F32) * (k < count[0, block]).astype(F32)).astype(BF16)
            for k in range(slots)
        ]
        left = jnp.concatenate(live, axis=1)
        picks = [index[0, block, k] for k in range(slots)]
        for c in range(tiles):
            col = pl.ds(c * TILE, TILE)
            right = jnp.concatenate([trans[pick, :, col] for pick in picks], axis=0)
            store(col, jnp.dot(left, right, preferred_element_type=F32))

    ups, downs = n_z - 1 - z, z
    both = jnp.minimum(ups, downs)

    def order(i):
        pair = i // 2
        one = jnp.where(i % 2 == 0, n_z - 1 - pair, pair)
        rest = jnp.where(ups > downs, n_z - 1 - i + both, i - both)
        d = jnp.where(i < 2 * both, one, rest)
        return jnp.where(i < n_z - 1, d, z)

    def x_copy(d, p):
        return to(peer_msg.at[d, p], x_in.at[d, p], x_send.at[d, p], x_recv.at[d, p], src=x_peer)

    if owned % BLK == 0:
        def peer_step(i):
            d, p = order(i // pieces), i % pieces

            def store(col, made):
                peer_msg[d, p, :, col] = made.astype(BF16)

            message((d * 2 + 1 - x) * pieces + p, store)
            x_copy(d, p).start()

        def own_step(i):
            d, p = order(i // pieces), i % pieces

            def store(col, made):
                own_msg[d, p, :, col] = made

            message((d * 2 + x) * pieces + p, store)

        pl.loop(0, n_z * pieces)(peer_step)
        pl.loop(0, n_z * pieces)(own_step)
    else:
        share = BLK // owned

        @pl.loop(0, tblocks)
        def _(block):
            def store(col, made):
                for e in range(share):
                    part = made[e * owned:(e + 1) * owned]
                    d = (block * share + e) // 2

                    @pl.when(x == e % 2)
                    def _():
                        own_msg[d, 0, :, col] = part

                    @pl.when(x != e % 2)
                    def _():
                        peer_msg[d, 0, :, col] = part.astype(BF16)

            message(block, store)

        @pl.loop(0, n_z)
        def _(i):
            x_copy(order(i), 0).start()

    def up_copy(d, p):
        return to(z_out.at[d, p], up_in.at[d, p], z_send.at[d, p], up_recv.at[d, p], src=s + 2)

    def down_copy(d, p):
        return to(z_out.at[d, p], down_in.at[d, p], z_send.at[d, p], down_recv.at[d, p], src=s - 2)

    def hop(d, p, copy, arrived, edge):
        x_copy(d, p).wait_recv()

        @pl.when(edge)
        def _():
            z_out[d, p] = (own_msg[d, p] + x_in[d, p].astype(F32)).astype(BF16)

        @pl.when(jnp.logical_not(edge))
        def _():
            copy(d, p).wait_recv()
            z_out[d, p] = (own_msg[d, p] + x_in[d, p].astype(F32) + arrived[d, p].astype(F32)).astype(BF16)

        copy(d, p).start()

    @pl.loop(0, n_z * pieces)
    def _(i):
        k, p = i // pieces, i % pieces
        pl.when(n_z - 1 - k > z)(lambda: hop(n_z - 1 - k, p, up_copy, up_in, z == 0))
        pl.when(k < z)(lambda: hop(k, p, down_copy, down_in, z == n_z - 1))

    @pl.loop(0, pieces)
    def _(p):
        x_copy(z, p).wait_recv()
        self_acc[p] = self_acc[p] + own_msg[z, p] + x_in[z, p].astype(F32)

        @pl.when(z > 0)
        def _():
            up_copy(z, p).wait_recv()
            self_acc[p] = self_acc[p] + up_in[z, p].astype(F32)

        @pl.when(z < n_z - 1)
        def _():
            down_copy(z, p).wait_recv()
            self_acc[p] = self_acc[p] + down_in[z, p].astype(F32)

        out[pl.ds(pl.multiple_of(p * piece, piece), piece), :] = jnp.maximum(self_acc[p], 0.0).astype(BF16)

    mate_copy.wait_send()
    for p in range(cuts):
        for j in range(1, n_y):
            y_copy(j, p, t, mate).wait_send()
            f_copy(j, p, t).wait_send()

    @pl.loop(0, n_z * pieces)
    def _(i):
        d, p = i // pieces, i % pieces
        x_copy(d, p).wait_send()
        pl.when(d != z)(lambda: up_copy(d, p).wait_send())


def shards(n_src, n_tgt, feat, tgt, rel, selfw, adj, index, count):
    rows, depth = feat.shape
    rels, _, hid = rel.shape
    _, tblocks, slots, _, _ = adj.shape
    owned = tgt.shape[0]
    n_z, n_y = n_src // 2, n_tgt // 2
    piece = min(BLK, owned)
    pieces = owned // piece
    cuts = 2
    dma = pltpu.SemaphoreType.DMA
    whole = pl.BlockSpec(memory_space=pl.ANY)
    scalar = pl.BlockSpec(memory_space=pltpu.SMEM)
    held = (n_z, pieces, piece, hid)
    total = n_tgt * rows
    return pl.pallas_call(
        functools.partial(kernel, n_src, n_tgt, cuts),
        out_shape=jax.ShapeDtypeStruct((owned, hid), BF16),
        in_specs=[whole] * 5 + [scalar] * 2,
        out_specs=pl.BlockSpec(memory_space=pltpu.VMEM),
        scratch_shapes=[
            pltpu.VMEM((n_tgt, rows, depth), BF16),
            pltpu.VMEM(rel.shape, BF16),
            pltpu.VMEM(selfw.shape, BF16),
            pltpu.VMEM(tgt.shape, BF16),
            pltpu.VMEM(adj.shape[1:], BF16),
            pltpu.VMEM((rels * total // BLK, BLK, hid), BF16),
            pltpu.VMEM((pieces, piece, hid), F32),
            pltpu.VMEM(held, BF16),
            pltpu.VMEM(held, F32),
            pltpu.VMEM(held, BF16),
            pltpu.VMEM(held, BF16),
            pltpu.VMEM(held, BF16),
            pltpu.VMEM(held, BF16),
            dma((5,)),
            dma((n_y - 1, cuts)), dma((n_y - 1, cuts)),
            dma, dma,
            dma((n_y - 1, cuts)), dma((n_y - 1, cuts)),
            dma((n_z, pieces)), dma((n_z, pieces)),
            dma((n_z, pieces)), dma((n_z, pieces)), dma((n_z, pieces)),
        ],
        compiler_params=pltpu.CompilerParams(
            collective_id=0, has_side_effects=True, vmem_limit_bytes=60 * 2**20),
        cost_estimate=pl.CostEstimate(
            flops=2 * rels * total * depth * hid + 2 * tblocks * slots * BLK * BLK * hid,
            bytes_accessed=2 * (rel.size + adj.size + feat.size), transcendentals=0),
    )(feat, tgt, rel, selfw, adj, index, count)


def solution(mesh):
    return jax.shard_map(
        functools.partial(shards, mesh.shape["src"], mesh.shape["tgt"]),
        mesh=mesh,
        in_specs=(
            P(("src", "tgt"), None),
            P(("tgt", "src"), None),
            P(),
            P(),
            P("src", "tgt", None, None, None),
            P("src", "tgt", None),
            P("src", "tgt"),
        ),
        out_specs=P(("tgt", "src"), None),
        check_vma=False,
    )
```

```python
import functools

import jax
import jax.numpy as jnp
from jax import lax
from jax.experimental import pallas as pl
from jax.experimental.pallas import tpu as pltpu
from jax.sharding import PartitionSpec as P

BLK = 128
TILE = 256
PART = 256
CUTS = 2
F32 = jnp.float32
BF16 = jnp.bfloat16


def kernel(n_src, n_tgt,
           feat, tgt, rel, selfw, adj, index, count, out,
           gath, rel_v, self_v, tgt_v, adj_v, live, trans, self_acc, peer_msg, own_msg, x_in, up_in, down_in, z_out,
           first_up, first_down, first_out,
           load_sem, y_send, y_recv, c_send, c_recv, f_send, f_recv, x_send, x_recv, z_send, up_recv, down_recv,
           first_send, first_up_recv, first_down_recv):
    s, t = lax.axis_index("src"), lax.axis_index("tgt")
    x, z = s % 2, s // 2
    y, core = t // 2, t % 2
    n_z = n_src // 2
    n_y, cuts, _, cut, depth = gath.shape
    mate = t + 1 - 2 * core
    x_peer = s + 1 - 2 * x
    rels, hid = rel_v.shape[0], rel_v.shape[2]
    rows = cuts * cut
    per_rel = trans.shape[0] // rels
    tblocks, slots = adj_v.shape[0], adj_v.shape[1]
    pieces, owned, part = z_out.shape[1], z_out.shape[2], z_out.shape[3]
    tiles = hid // TILE
    halves = TILE // part
    edge = (z == 0) | (z == n_z - 1)

    def to(src_ref, dst_ref, send, recv, **where):
        return pltpu.make_async_remote_copy(
            src_ref=src_ref, dst_ref=dst_ref, send_sem=send, recv_sem=recv,
            device_id=where, device_id_type=pl.DeviceIdType.MESH)

    def features(p):
        return feat.at[pl.ds(p * cut, cut)]

    loads = [
        pltpu.make_async_copy(rel, rel_v, load_sem.at[0]),
        pltpu.make_async_copy(tgt, tgt_v, load_sem.at[1]),
        pltpu.make_async_copy(selfw, self_v, load_sem.at[2]),
        pltpu.make_async_copy(adj.at[0], adj_v, load_sem.at[3]),
    ] + [
        pltpu.make_async_copy(features(p), gath.at[y, p, core], load_sem.at[4 + p])
        for p in range(cuts)
    ]
    for load in loads:
        load.start()

    barrier = pltpu.get_barrier_semaphore()

    def greet(**where):
        pl.semaphore_signal(barrier, inc=1, device_id=where, device_id_type=pl.DeviceIdType.MESH)

    greet(tgt=mate)
    greet(src=x_peer)
    for j in range(1, n_y):
        greet(tgt=(t + 2 * j) % n_tgt)
    pl.when(z > 0)(lambda: greet(src=s - 2))
    pl.when(z < n_z - 1)(lambda: greet(src=s + 2))
    pl.semaphore_wait(barrier, n_y + 1 + jnp.minimum(z, 1) + jnp.minimum(n_z - 1 - z, 1))

    def y_copy(j, p, owner, peer):
        return to(features(p), gath.at[owner, p, core], y_send.at[j - 1, p], y_recv.at[j - 1, p], tgt=peer)

    def f_copy(j, p, owner):
        here = gath.at[owner, p, core]
        return to(here, here, f_send.at[j - 1, p], f_recv.at[j - 1, p], tgt=mate)

    def mate_copy(p):
        return to(features(p), gath.at[y, p, core], c_send.at[p], c_recv.at[p], tgt=mate)

    for p in range(cuts):
        for j in range(1, n_y):
            y_copy(j, p, y, (t + 2 * j) % n_tgt).start()
    for p in range(cuts):
        mate_copy(p).start()

    def transform(owner, p, c):
        col = pl.ds(pl.multiple_of(c * TILE, TILE), TILE)
        many = cut // BLK
        block = (2 * owner * rows + p * cut) // BLK
        for r in range(rels):
            made = jnp.dot(gath[owner, p].reshape(2 * cut, depth), rel_v[r, :, col], preferred_element_type=F32)
            made = made.astype(BF16).reshape(2, many, BLK, TILE)
            trans[pl.ds(r * per_rel + block, many), :, col] = made[0]
            trans[pl.ds(r * per_rel + block + rows // BLK, many), :, col] = made[1]

    loads[0].wait()
    for p in range(cuts):
        loads[4 + p].wait()
        mate_copy(p).wait_recv()
        pl.loop(0, tiles)(lambda c: transform(y, p, c))
    for load in loads[1:4]:
        load.wait()

    @pl.loop(0, tiles)
    def _(c):
        col = pl.ds(pl.multiple_of(c * TILE, TILE), TILE)
        made = jnp.dot(tgt_v[...], self_v[:, col], preferred_element_type=F32)
        for h in range(halves):
            self_acc[c * halves + h] = made[:, h * part:(h + 1) * part]

    @pl.loop(0, tblocks)
    def _(block):
        for k in range(slots):
            keep = (k < count[0, block]).astype(F32)
            live[block, :, k * BLK:(k + 1) * BLK] = (adj_v[block, k].astype(F32) * keep).astype(BF16)

    def arrive(p):
        for j in range(1, n_y):
            owner = (y - j + n_y) % n_y
            y_copy(j, p, owner, t).wait_recv()
            f_copy(j, p, owner).start()
        for j in range(1, n_y):
            f_copy(j, p, (y - j + n_y) % n_y).wait_recv()

    for p in range(cuts - 1):
        arrive(p)
        for j in range(1, n_y):
            pl.loop(0, tiles)(lambda c: transform((y - j + n_y) % n_y, p, c))
    arrive(cuts - 1)

    def message(block, c):
        col = pl.ds(pl.multiple_of(c * TILE, TILE), TILE)
        right = jnp.concatenate([trans[index[0, block, k], :, col] for k in range(slots)], axis=0)
        return jnp.dot(live[block], right, preferred_element_type=F32)

    ups, downs = n_z - 1 - z, z
    both = jnp.minimum(ups, downs)

    def order(i):
        pair = i // 2
        one = jnp.where(i % 2 == 0, n_z - 1 - pair, pair)
        rest = jnp.where(ups > downs, n_z - 1 - i + both, i - both)
        d = jnp.where(i < 2 * both, one, rest)
        return jnp.where(i < n_z - 1, d, z)

    def x_copy(d, p):
        return to(peer_msg.at[d, p], x_in.at[d, p], x_send.at[d, p], x_recv.at[d, p], src=x_peer)

    def first_copy(d, side, way):
        here = first_out.at[d, side]
        if way == 0:
            return to(here, first_up.at[d, side], first_send.at[d, side], first_up_recv.at[d, side], src=s + 2)
        return to(here, first_down.at[d, side], first_send.at[d, side], first_down_recv.at[d, side], src=s - 2)

    def start_x(d, c):
        for h in range(halves):
            p = c * halves + h
            pl.when(p > 0)(lambda: x_copy(d, p).start())

    def aggregate(c):
        if owned % BLK == 0:
            many = owned // BLK

            def build(d, side, place):
                for b in range(many):
                    made = message((d * 2 + side) * many + b, c)
                    for h in range(halves):
                        got = made[:, h * part:(h + 1) * part].astype(place.dtype)
                        place[d, c * halves + h, b * BLK:(b + 1) * BLK, :] = got

            @pl.loop(0, n_z)
            def _(i):
                d = order(i)
                build(d, 1 - x, peer_msg)
                start_x(d, c)

            pl.loop(0, n_z)(lambda i: build(order(i), x, own_msg))
        else:
            share = BLK // owned

            @pl.loop(0, tblocks)
            def _(block):
                made = message(block, c)
                for e in range(share):
                    d = (block * share + e) // 2
                    for h in range(halves):
                        got = made[e * owned:(e + 1) * owned, h * part:(h + 1) * part]

                        @pl.when(x == e % 2)
                        def _():
                            own_msg[d, c * halves + h] = got

                        @pl.when(x != e % 2)
                        def _():
                            peer_msg[d, c * halves + h] = got.astype(BF16)

            pl.loop(0, n_z)(lambda i: start_x(order(i), c))

    @pl.loop(0, tiles)
    def _(c):
        for j in range(1, n_y):
            transform((y - j + n_y) % n_y, cuts - 1, c)
        aggregate(c)

        @pl.when((c == 0) & edge)
        def _():
            @pl.loop(0, n_z - 1)
            def _(i):
                d = order(i)
                first_out[d, 0] = own_msg[d, 0].astype(BF16)
                first_out[d, 1] = peer_msg[d, 0]
                for side in range(2):
                    pl.when(z == 0)(lambda: first_copy(d, side, 0).start())
                    pl.when(z > 0)(lambda: first_copy(d, side, 1).start())

    def first_hop(d, way, arrived):
        for side, held in ((0, own_msg), (1, peer_msg)):
            copy = first_copy(d, side, way)
            copy.wait_recv()
            first_out[d, side] = (held[d, 0].astype(F32) + arrived[d, side].astype(F32)).astype(BF16)
            copy.start()

    def up_copy(d, p):
        return to(z_out.at[d, p], up_in.at[d, p], z_send.at[d, p], up_recv.at[d, p], src=s + 2)

    def down_copy(d, p):
        return to(z_out.at[d, p], down_in.at[d, p], z_send.at[d, p], down_recv.at[d, p], src=s - 2)

    def hop(d, p, copy, arrived, last):
        x_copy(d, p).wait_recv()

        @pl.when(last)
        def _():
            z_out[d, p] = (own_msg[d, p] + x_in[d, p].astype(F32)).astype(BF16)

        @pl.when(jnp.logical_not(last))
        def _():
            copy(d, p).wait_recv()
            z_out[d, p] = (own_msg[d, p] + x_in[d, p].astype(F32) + arrived[d, p].astype(F32)).astype(BF16)

        copy(d, p).start()

    def finish(p, total):
        total = total + x_in[z, p].astype(F32)
        out[:, pl.ds(pl.multiple_of(p * part, part), part)] = jnp.maximum(total, 0.0).astype(BF16)

    def close(p):
        self_acc[p] = self_acc[p] + own_msg[z, p]

        @pl.when(z > 0)
        def _():
            up_copy(z, p).wait_recv()
            self_acc[p] = self_acc[p] + up_in[z, p].astype(F32)

        @pl.when(z < n_z - 1)
        def _():
            down_copy(z, p).wait_recv()
            self_acc[p] = self_acc[p] + down_in[z, p].astype(F32)

        x_copy(z, p).wait_recv()
        finish(p, self_acc[p])

    def cross():
        self_acc[0] = self_acc[0] + own_msg[z, 0]
        own_msg[z, 0] = peer_msg[z, 0].astype(F32)
        for reached, way, arrived in ((z > 0, 0, first_up), (z < n_z - 1, 1, first_down)):
            @pl.when(reached)
            def _():
                for side in range(2):
                    first_copy(z, side, way).wait_recv()
                self_acc[0] = self_acc[0] + arrived[z, 0].astype(F32)
                own_msg[z, 0] = own_msg[z, 0] + arrived[z, 1].astype(F32)
        peer_msg[z, 0] = own_msg[z, 0].astype(BF16)
        x_copy(z, 0).start()

    @pl.loop(0, pieces + n_z)
    def _(i):
        up, down = i - z, i - (n_z - 1 - z)

        @pl.loop(0, n_z)
        def _(k):
            far = n_z - 1 - k

            @pl.when(far > z)
            def _():
                pl.when((up == 0) & jnp.logical_not(edge))(lambda: first_hop(far, 0, first_up))
                pl.when((up > 0) & (up < pieces))(lambda: hop(far, up, up_copy, up_in, z == 0))

            @pl.when(k < z)
            def _():
                pl.when((down == 0) & jnp.logical_not(edge))(lambda: first_hop(k, 1, first_down))
                pl.when((down > 0) & (down < pieces))(lambda: hop(k, down, down_copy, down_in, z == n_z - 1))

        pl.when(i == n_z)(cross)
        pl.when(i > n_z)(lambda: close(i - n_z))

    x_copy(z, 0).wait_recv()
    finish(0, self_acc[0])

    for p in range(cuts):
        mate_copy(p).wait_send()
        for j in range(1, n_y):
            y_copy(j, p, y, mate).wait_send()
            f_copy(j, p, y).wait_send()

    @pl.loop(0, n_z)
    def _(d):
        @pl.when(d != z)
        def _():
            for side in range(2):
                first_copy(d, side, 0).wait_send()

        pl.when(d == z)(lambda: x_copy(d, 0).wait_send())

        @pl.loop(1, pieces)
        def _(p):
            x_copy(d, p).wait_send()
            pl.when(d != z)(lambda: up_copy(d, p).wait_send())


def shards(n_src, n_tgt, feat, tgt, rel, selfw, adj, index, count):
    rows, depth = feat.shape
    rels, _, hid = rel.shape
    _, tblocks, slots, _, _ = adj.shape
    owned = tgt.shape[0]
    n_z, n_y = n_src // 2, n_tgt // 2
    pieces = hid // PART
    cuts = CUTS
    dma = pltpu.SemaphoreType.DMA
    whole = pl.BlockSpec(memory_space=pl.ANY)
    scalar = pl.BlockSpec(memory_space=pltpu.SMEM)
    held = (n_z, pieces, owned, PART)
    first = (n_z, 2, owned, PART)
    total = n_tgt * rows
    return pl.pallas_call(
        functools.partial(kernel, n_src, n_tgt),
        out_shape=jax.ShapeDtypeStruct((owned, hid), BF16),
        in_specs=[whole] * 5 + [scalar] * 2,
        out_specs=pl.BlockSpec(memory_space=pltpu.VMEM),
        scratch_shapes=[
            pltpu.VMEM((n_y, cuts, 2, rows // cuts, depth), BF16),
            pltpu.VMEM(rel.shape, BF16),
            pltpu.VMEM(selfw.shape, BF16),
            pltpu.VMEM(tgt.shape, BF16),
            pltpu.VMEM(adj.shape[1:], BF16),
            pltpu.VMEM((tblocks, BLK, slots * BLK), BF16),
            pltpu.VMEM((rels * total // BLK, BLK, hid), BF16),
            pltpu.VMEM((pieces, owned, PART), F32),
            pltpu.VMEM(held, BF16),
            pltpu.VMEM(held, F32),
            pltpu.VMEM(held, BF16),
            pltpu.VMEM(held, BF16),
            pltpu.VMEM(held, BF16),
            pltpu.VMEM(held, BF16),
            pltpu.VMEM(first, BF16),
            pltpu.VMEM(first, BF16),
            pltpu.VMEM(first, BF16),
            dma((4 + cuts,)),
            dma((n_y - 1, cuts)), dma((n_y - 1, cuts)),
            dma((cuts,)), dma((cuts,)),
            dma((n_y - 1, cuts)), dma((n_y - 1, cuts)),
            dma((n_z, pieces)), dma((n_z, pieces)),
            dma((n_z, pieces)), dma((n_z, pieces)), dma((n_z, pieces)),
            dma((n_z, 2)), dma((n_z, 2)), dma((n_z, 2)),
        ],
        compiler_params=pltpu.CompilerParams(
            collective_id=0, has_side_effects=True, vmem_limit_bytes=60 * 2**20),
        cost_estimate=pl.CostEstimate(
            flops=2 * rels * total * depth * hid + 2 * tblocks * slots * BLK * BLK * hid,
            bytes_accessed=2 * (rel.size + adj.size + feat.size), transcendentals=0),
    )(feat, tgt, rel, selfw, adj, index, count)


def solution(mesh):
    return jax.shard_map(
        functools.partial(shards, mesh.shape["src"], mesh.shape["tgt"]),
        mesh=mesh,
        in_specs=(
            P(("src", "tgt"), None),
            P(("tgt", "src"), None),
            P(),
            P(),
            P("src", "tgt", None, None, None),
            P("src", "tgt", None),
            P("src", "tgt"),
        ),
        out_specs=P(("tgt", "src"), None),
        check_vma=False,
    )
```
